1024 devices in a mesh: dp: 16 (over y, core), expert: 64 (over x, z).
Axes of the slice: x: 4, y: 8, z: 16, core: 2. Of those that a mesh axis runs over, the one named last changes fastest.
Arguments:
- tokens: bfloat16 [8192, 4096], P('expert', 'dp'), may hold values from -6 to 6
- out_grad: bfloat16 [8192, 4096], P('expert', 'dp'), may hold values from -6 to 6
- route_expert: int32 [8192, 2], P('expert'), may hold values from 0 to 63, all different within a row; in each aligned block of 128 rows (0 to 127, 128 to 255, ...) at most 8 rows name the same one
- route_weight: float32 [8192, 2], P('expert'), may hold values from 0.1 to 1
- gate_weight: bfloat16 [64, 4096, 768], P('expert', 'dp'), may hold values from -0.09375 to 0.09375
- up_weight: bfloat16 [64, 4096, 768], P('expert', 'dp'), may hold values from -0.09375 to 0.09375
- down_weight: bfloat16 [64, 768, 4096], P('expert', None, 'dp'), may hold values from -0.21875 to 0.21875
Outputs:
- grad_tokens: float32 [8192, 4096], P('expert', 'dp')
- grad_gate: bfloat16 [64, 4096, 768], P('expert', 'dp')
- grad_up: bfloat16 [64, 4096, 768], P('expert', 'dp')
- grad_down: bfloat16 [64, 768, 4096], P('expert', None, 'dp')
The draws below stay inside these ranges and needn't reach their ends.
Inputs may be any that keep to these rules, and one draw needn't show every extreme that they name: `route_expert`: each token's 2 experts differ; among the tokens of one index of the expert axis (aligned blocks of 128 tokens) no expert is named by more than 8 routes, a bound that some block reaches.
All inputs are finite; a program needn't handle non-finite values.
Results may differ from the reference program's by a relative error of at most 0.0057.
Values may be sent and summed in bfloat16 or wider, within the bound.
A program may use at most 32 MiB of HBM per device.

```python
import math
import jax
import jax.numpy as jnp
import numpy as np
from jax import lax

D = 4096
H = 768
TOPK = 2
TOK_DEV = 128
EXPERTS = 64
CAP = 8
TOKENS = 8192


def level_of(own_key, shape, shards, least, largest):
    level, own = 1.0, jax.random.fold_in(own_key, 6)
    for dim, parts in shards:
        draws = jnp.exp(jax.random.uniform(jax.random.fold_in(own, dim), (parts,), jnp.float32, least / len(shards), largest / len(shards)))
        level = level * jnp.repeat(draws, shape[dim] // parts).reshape([-1 if axis == dim else 1 for axis in range(len(shape))])
    return level


def deal_out(stream_key, own, number, rows, count, top, limit, skew):
    ranking = jax.random.permutation(stream_key, count)
    crowded, common = portions_of(count, rows * top, limit, skew, True), portions_of(count, rows * top, limit, skew, False)
    places = jnp.arange(count)

    def named(sizes, rotation):
        used = int((sizes > 0).sum())
        fixed = max(1, used // 4)
        moved = fixed + (places - fixed + rotation * (used - fixed)) % max(1, count - fixed)
        return jnp.zeros((count,), jnp.int32).at[ranking[jnp.where(places < fixed, places, moved)]].set(jnp.asarray(sizes, jnp.int32))

    sizes = jnp.where(number % 4 == 0, named(crowded, number // 4), named(common, number - number // 4 - 1))
    mixed = jax.random.permutation(jax.random.fold_in(own, 3), count)
    giver, receiver = mixed[0:count // 2 * 2:2], mixed[1:count // 2 * 2:2]
    room = jnp.minimum(sizes[giver] - 1, limit - sizes[receiver]) // 2
    room = jnp.where((giver == ranking[0]) | (receiver == ranking[0]) | (sizes[receiver] == 0), 0, jnp.maximum(room, 0))
    moved = jax.random.randint(jax.random.fold_in(own, 4), (count // 2,), 0, 1 << 20) % (room + 1)
    sizes = sizes.at[giver].add(-moved).at[receiver].add(moved)
    items = jnp.searchsorted(jnp.cumsum(sizes), jnp.arange(rows * top), side="right").astype(jnp.int32)
    table = items.reshape(top, rows).T
    table = table[jax.random.permutation(jax.random.fold_in(own, 1), rows)]
    rotation = jax.random.randint(jax.random.fold_in(own, 2), (rows, 1), 0, top)
    return jnp.take_along_axis(table, (jnp.arange(top)[None, :] + rotation) % top, axis=1)


def portions_of(number_of, total, reach, skew, full):
    weights = [(1 << 20) // math.isqrt(rank ** skew) + 1 for rank in range(1, number_of + 1)]
    largest = reach if full else min(reach, max(-(-total // number_of), total * weights[0] // sum(weights)))
    least = 1 if total - largest >= number_of - 1 else 0
    given, rest = [largest] + [least] * (number_of - 1), total - largest - least * (number_of - 1)
    while rest > 0:
        movable = [i for i in range(1, number_of) if given[i] < largest] or [i for i in range(1, number_of) if given[i] < reach]
        whole, budget = sum([weights[i] for i in movable]), rest
        for i in movable:
            more = min(reach - given[i], max(1, budget * weights[i] // whole), rest)
            given[i] = given[i] + more
            rest = rest - more
    return np.array(given)


def bell_draw(rng, extent, deviation, bound, shards=(), kind=jnp.bfloat16):
    factor_of = level_of(rng, extent, shards, -0.22, 0.18) if shards else 1.0
    values = jax.random.normal(rng, extent, jnp.float32) * deviation * factor_of
    return jnp.minimum(jnp.maximum(values, -bound), bound).astype(kind)


def setup_inputs(seed: int = 0) -> dict:
    splits = jax.random.split(jax.random.key(seed), 8)
    tokens = bell_draw(splits[0], (TOKENS, D), 1.0, 6.0, ((0, 64), (1, 16)))
    out_grad = bell_draw(splits[1], (TOKENS, D), 1.0, 6.0, ((0, 64), (1, 16)))
    route_expert_keys = jax.random.split(jax.random.fold_in(splits[2], 1), TOKENS // TOK_DEV)
    route_expert_turns = jax.random.permutation(jax.random.fold_in(splits[2], 3), TOKENS // TOK_DEV)
    route_expert = jax.vmap(lambda own, number: deal_out(jax.random.fold_in(splits[2], 2), own, number, TOK_DEV, EXPERTS, TOPK, CAP, 2))(route_expert_keys, route_expert_turns).reshape((TOKENS, TOPK))
    route_weight = jnp.clip(0.1 + 0.9 * jax.random.uniform(splits[3], (TOKENS, TOPK), jnp.float32) ** level_of(splits[3], (TOKENS, TOPK), ((0, 64),), -0.2, 0.2), 0.1, 1.0)
    gate_weight = bell_draw(splits[4], (EXPERTS, D, H), D ** -0.5, 0.09375, ((0, 64), (1, 16)))
    up_weight = bell_draw(splits[5], (EXPERTS, D, H), D ** -0.5, 0.09375, ((0, 64), (1, 16)))
    down_weight = bell_draw(splits[6], (EXPERTS, H, D), H ** -0.5, 0.21875, ((0, 64), (2, 16)))
    return dict(tokens=tokens, out_grad=out_grad, route_expert=route_expert, route_weight=route_weight, gate_weight=gate_weight, up_weight=up_weight, down_weight=down_weight)


def reference(tokens, out_grad, route_expert, route_weight, gate_weight, up_weight, down_weight):
    block = TOK_DEV * TOPK
    slots = EXPERTS * CAP
    route_count = TOKENS * TOPK
    groups_all = TOKENS // TOK_DEV
    flat_expert = route_expert.reshape(route_count).astype(jnp.int32)
    route_order = jnp.arange(route_count, dtype=jnp.int32)
    token_of = route_order // TOPK
    group_of = route_order // block
    blocked = flat_expert.reshape(groups_all, block)
    inner = jnp.arange(block, dtype=jnp.int32)
    earlier = inner[None, :] < inner[:, None]
    matches = (blocked[:, :, None] == blocked[:, None, :]) & earlier[None, :, :]
    slot_rank = jnp.sum(matches.astype(jnp.int32), axis=2).reshape(route_count)
    position = (flat_expert * slots + group_of * CAP + slot_rank).astype(jnp.int32)
    table = jnp.zeros((EXPERTS * slots,), jnp.int32).at[position].set(route_order + 1)
    table = table.reshape(EXPERTS, slots)
    scaled = (route_weight.reshape(route_count)[:, None] * out_grad[token_of].astype(jnp.float32)).astype(jnp.bfloat16)

    def one_expert(items):
        entries, w_gate, w_up, w_down = items
        live = (entries > 0)[:, None]
        source = jnp.maximum(entries - 1, 0).astype(jnp.int32)
        x_rows = jnp.where(live, tokens[token_of[source]], jnp.zeros((), tokens.dtype))
        g_rows = jnp.where(live, scaled[source], jnp.zeros((), scaled.dtype))
        gate = jnp.dot(x_rows, w_gate, preferred_element_type=jnp.float32)
        upper = jnp.dot(x_rows, w_up, preferred_element_type=jnp.float32)
        d_act = jnp.dot(g_rows, w_down.T, preferred_element_type=jnp.float32)
        sigma = jax.nn.sigmoid(gate)
        silu_value = gate * sigma
        activation = (silu_value * upper).astype(jnp.bfloat16)
        d_gate = (d_act * upper * sigma * (1.0 + gate * (1.0 - sigma))).astype(jnp.bfloat16)
        d_up = (d_act * silu_value).astype(jnp.bfloat16)
        grad_down = jnp.dot(activation.T, g_rows, preferred_element_type=jnp.float32).astype(jnp.bfloat16)
        grad_gate = jnp.dot(x_rows.T, d_gate, preferred_element_type=jnp.float32).astype(jnp.bfloat16)
        grad_up = jnp.dot(x_rows.T, d_up, preferred_element_type=jnp.float32).astype(jnp.bfloat16)
        d_rows = (jnp.dot(d_gate, w_gate.T, preferred_element_type=jnp.float32)
                  + jnp.dot(d_up, w_up.T, preferred_element_type=jnp.float32)).astype(jnp.bfloat16)
        return grad_gate, grad_up, grad_down, d_rows

    grad_gate, grad_up, grad_down, d_rows = lax.map(one_expert, (table, gate_weight, up_weight, down_weight))
    route_grads = d_rows.reshape(EXPERTS * slots, D)[position].astype(jnp.float32)
    grad_tokens = jnp.sum(route_grads.reshape(TOKENS, TOPK, D), axis=1)
    return grad_tokens, grad_gate, grad_up, grad_down
```

```python
import functools

import jax
import jax.numpy as jnp
from jax import lax
from jax.experimental import pallas as pl
from jax.experimental.pallas import tpu as pltpu
from jax.sharding import PartitionSpec as P

MESH = pl.DeviceIdType.MESH
NX, NZ, NY = 4, 16, 8
EXPERTS = NX * NZ
TOK, FEAT, HID, CAP = 128, 256, 768, 8
HALF = HID // 2
CHUNKS = 8
SRC = EXPERTS // 2 // CHUNKS
ROWS = SRC * CAP
MINE = CHUNKS * ROWS
LONG, SHORT = NY // 2, NY // 2 - 1
DZ = ((1, 15), (2, 14), (7, 9), (6, 10), (0, 8), (5, 11), (4, 12), (3, 13))
DIRECT = (7,)
DEPTH = 3
ARRIVE = (5, 9, 16, 20, 24, 26, 28, 30)
TWO_STEPS = dict(D=0, B=4.7, F=9.5, H=14.5, E=19)
ONE_STEP = dict(D=0, F=6.5, E=13)
ORDER = sorted(
    (ARRIVE[k] + after, k, name)
    for k in range(CHUNKS)
    for name, after in (ONE_STEP if k in DIRECT else TWO_STEPS).items()
)
VMEM_LIMIT = 60 * 1024 * 1024
F32, BF16 = jnp.float32, jnp.bfloat16


def dot(a, b, ca, cb):
    return lax.dot_general(a, b, (((ca,), (cb,)), ((), ())), preferred_element_type=F32)


def kernel(
    tok_hbm, og_hbm, rexp_hbm, rwt_hbm, wg, wu, wd,
    g_tok_hbm, g_gate_hbm, g_up_hbm, g_down_hbm,
    tok, og, rexp, rwt, g_tok, g_gate, g_up, g_down,
    wgu, wdn, send, qt, rx, xs, part, out_blocks, in_blocks, dall, rsend, ret, xall, gall,
    a_sem, o_sem, w_sem, ws_send, ws_recv, d_send, d_recv, x_send, x_recv,
    rs_send, rs_recv, ag_send, ag_recv, sh_send, sh_recv, r_send, r_recv,
):
    dp, ex = lax.axis_index("dp"), lax.axis_index("expert")
    y, c = lax.div(dp, 2), lax.rem(dp, 2)
    x, z = lax.div(ex, NZ), lax.rem(ex, NZ)
    sib = (y * 2 + 1 - c, ex)
    sigma = 1 - 2 * c

    small = [
        pltpu.make_async_copy(s, d, a_sem.at[i])
        for i, (s, d) in enumerate([(rexp_hbm, rexp), (rwt_hbm, rwt), (tok_hbm, tok), (og_hbm, og)])
    ]
    for copy in small:
        copy.start()

    x_at = [lax.rem(x + dx, NX) * NZ for dx in range(NX)]
    z_at = [lax.rem(z + dz, NZ) for dz in range(NZ)]
    y_at = {n: lax.rem(y + n * sigma + NY, NY) for n in range(-SHORT, LONG + 1)}
    x_even = [lax.rem(x + c + 2 * i, NX) * NZ for i in range(2)]
    x_odd = [lax.rem(x + 1 - c + 2 * i, NX) * NZ for i in range(2)]
    x_back = [lax.rem(x + 2 * NX - c - 2 * i, NX) * NZ for i in range(2)]

    def along_y(n):
        return (y_at[n] * 2 + c, ex)

    barrier = pltpu.get_barrier_semaphore()

    def signal(target):
        pl.semaphore_signal(barrier, inc=1, device_id=target, device_id_type=MESH)

    for dz in [8, 7, 9, 6, 10, 5, 11, 4, 12, 3, 13, 2, 14, 1, 15, 0]:
        for i in range(2):
            if dz == 0 and i == 0:
                pl.when(c == 1)(lambda: signal((y * 2, x_even[0] + z_at[0])))
            else:
                signal((y * 2, x_even[i] + z_at[dz]))
            signal((y * 2 + 1, x_even[i] + z_at[dz]))
            signal((y * 2 + 1 - c, x_odd[i] + z_at[dz]))
    for n in (4, 3, -3, 2, -2, 1, -1):
        signal(along_y(n))

    own_cols = pl.ds(pl.multiple_of(c * FEAT, FEAT), FEAT)
    sib_cols = pl.ds(pl.multiple_of((1 - c) * FEAT, FEAT), FEAT)

    def weight_parts():
        for hh in range(2):
            h_cols = pl.ds(hh * HALF, HALF)
            yield wg.at[0, :, h_cols], wgu.at[hh, own_cols, pl.ds(0, HALF)]
            yield wu.at[0, :, h_cols], wgu.at[hh, own_cols, pl.ds(HALF, HALF)]
        yield wd.at[0], wdn.at[:, own_cols]

    w_local = [pltpu.make_async_copy(s, d, w_sem.at[i]) for i, (s, d) in enumerate(weight_parts())]
    for copy in w_local:
        copy.start()
    for copy in small:
        copy.wait()

    lane = lax.broadcasted_iota(jnp.int32, (TOK, TOK), 1)
    sub = lax.broadcasted_iota(jnp.int32, (TOK, TOK), 0)
    ef, w = rexp[...].astype(F32), rwt[...]
    e0r, e1r = ef[0:1, :], ef[1:2, :]
    columns = jnp.where(
        sub == 0, e0r, jnp.where(sub == 1, e1r, jnp.where(sub == 2, w[0:1, :], w[1:2, :]))
    ).T
    e0c, e1c, w0c, w1c = columns[:, 0:1], columns[:, 1:2], columns[:, 2:3], columns[:, 3:4]
    slots = 2 * EXPERTS * CAP
    si = lax.broadcasted_iota(jnp.int32, (slots, TOK), 0)
    s_exp = (si // (2 * CAP)).astype(F32)
    s_rank = (si % CAP).astype(F32)
    s_cot = (si % (2 * CAP)) >= CAP
    m0 = (s_exp == e0r).astype(F32)
    m1 = (s_exp == e1r).astype(F32)
    rank = dot((m0 + m1).astype(BF16), (sub < lane).astype(BF16), 1, 0)
    hit = rank == s_rank
    zero = jnp.zeros_like(m0)
    p0 = jnp.where(hit, m0, zero)
    p1 = jnp.where(hit, m1, zero)
    onehot = jnp.concatenate(
        [jnp.where(s_cot, zero, p0 + p1), jnp.where(s_cot, p0, zero), jnp.where(s_cot, p1, zero)], axis=1
    ).astype(BF16)
    o = og[...].astype(F32)
    g0 = (w0c * o).astype(BF16)
    g1 = (w1c * o).astype(BF16)
    values = jnp.concatenate([tok[...], g0, g1], axis=0)
    send[...] = dot(onehot, values, 1, 0).astype(BF16)

    pl.semaphore_wait(barrier, 102 + c)

    def dispatch(k):
        for j, dz in enumerate(DZ[k]):
            for dx in range(NX):
                target = x_at[dx] + z_at[dz]
                src = send.at[pl.ds(pl.multiple_of(target * 16, 16), 16), :]
                dst = rx.at[k, pl.ds((j * 2 + dx // 2) * 16, 16), own_cols]
                copy = pltpu.make_async_remote_copy(
                    src, dst, d_send, d_recv.at[k],
                    device_id=(y * 2 + dx % 2, target), device_id_type=MESH,
                )
                if dx == 0 and dz == 0:
                    pl.when(c == 0)(pltpu.make_async_copy(src, dst, d_recv.at[k]).start)
                    pl.when(c == 1)(copy.start)
                else:
                    copy.start()

    dispatch(0)
    w_remote = [
        pltpu.make_async_remote_copy(
            s, d, ws_send.at[i], ws_recv.at[i], device_id=sib, device_id_type=MESH
        )
        for i, (s, d) in enumerate(weight_parts())
    ]
    for copy in w_remote:
        copy.start()
    for k in range(1, DEPTH):
        dispatch(k)

    ti = lax.broadcasted_iota(jnp.int32, (TOK, slots), 1)
    t_exp = (ti // (2 * CAP)).astype(F32)
    t_rank = (ti % CAP).astype(F32)
    t_cot = (ti % (2 * CAP)) >= CAP
    tm = (t_exp == e0c).astype(F32) + (t_exp == e1c).astype(F32)
    trank = dot((lane < sub).astype(BF16), tm.astype(BF16), 1, 0)
    tz = jnp.zeros_like(tm)
    tp = jnp.where(trank == t_rank, tm, tz)
    qt[0:TOK, :] = jnp.where(t_cot, tz, tp).astype(BF16)
    qt[TOK:, :] = jnp.where(t_cot, tp, tz).astype(BF16)

    for copy in w_local:
        copy.wait()

    def whole(ref, sem):
        pltpu.make_async_copy(ref, ref, sem).wait()

    def split(rows16):
        v = rows16.astype(F32)
        width = v.shape[1]
        v = v.reshape(SRC, 2, CAP, width)
        return v[:, 0].reshape(ROWS, width).astype(BF16), v[:, 1].reshape(ROWS, width).astype(BF16)

    def rows_of(blocks):
        return blocks.astype(F32).reshape(blocks.shape[0] * CAP, blocks.shape[2]).astype(BF16)

    RS_TO = [2, 1, -1, 1, -1, 2, -2]
    RS_FOR = [4, 3, -3, 1, -1, 2, -2]
    RS_ADD = {5: (0, 1), 6: (2,)}
    FAR_FIRST = [4, 3, -3, 2, -2, 1, -1]

    def block(k, n):
        return part[k, pl.ds(pl.multiple_of(y_at[n] * 8, 8), 8), :]

    def rs(k, m):
        return pltpu.make_async_remote_copy(
            out_blocks.at[k, m], in_blocks.at[k, m], rs_send, rs_recv.at[k, m],
            device_id=along_y((FAR_FIRST if k in DIRECT else RS_TO)[m]), device_id_type=MESH,
        )

    AG_TO = [2, -2, 1, -1, 1, 2, -1]
    AG_OF = [0, 0, 0, 0, -2, -2, 2]

    def home(k, n):
        who = y_at[n]
        return dall.at[lax.div(who, 4), (c * CHUNKS + k) * 4 + lax.rem(who, 4)]

    def ag(k, m):
        ref = home(k, 0 if k in DIRECT else AG_OF[m])
        to = along_y((FAR_FIRST if k in DIRECT else AG_TO)[m])
        return pltpu.make_async_remote_copy(
            ref, ref, ag_send, ag_recv.at[k, m], device_id=to, device_id_type=MESH
        )

    def x_share(k):
        return pltpu.make_async_remote_copy(
            rx.at[k, :, sib_cols], xs.at[k], x_send, x_recv.at[k], device_id=sib, device_id_type=MESH
        )

    def own_rows(k):
        return pl.ds(pl.multiple_of(c * MINE + k * ROWS, ROWS), ROWS)

    def sib_rows(k):
        return pl.ds(pl.multiple_of((1 - c) * MINE + k * ROWS, ROWS), ROWS)

    def own_blocks(k):
        return pl.ds((c * CHUNKS + k) * 4, 4)

    def d_share(k):
        ref = dall.at[:, own_blocks(k)]
        return pltpu.make_async_remote_copy(
            ref, ref, sh_send, sh_recv.at[k], device_id=sib, device_id_type=MESH
        )

    def stage_first(k):
        whole(rx.at[k], d_recv.at[k])
        if k + DEPTH < CHUNKS:
            dispatch(k + DEPTH)
        x_share(k).start()
        if k == 0:
            for copy in w_remote:
                copy.wait_recv()
        xv, gv = split(rx[k])
        for hh in range(2):
            part[k, hh * ROWS:(hh + 1) * ROWS, 0:HID] = dot(xv, wgu[hh], 1, 0)
            part[k, hh * ROWS:(hh + 1) * ROWS, HID:] = dot(gv, wdn[hh * HALF:(hh + 1) * HALF, :], 1, 1)
        for m in range(7 if k in DIRECT else 5):
            out_blocks[k, m] = block(k, (FAR_FIRST if k in DIRECT else RS_FOR)[m]).astype(BF16)
            rs(k, m).start()

    def stage_relay(k):
        for m in (5, 6):
            acc = block(k, RS_FOR[m])
            for n in RS_ADD[m]:
                rs(k, n).wait_recv()
                acc = acc + in_blocks[k, n].astype(F32)
            out_blocks[k, m] = acc.astype(BF16)
            rs(k, m).start()

    def stage_point(k):
        acc = block(k, 0)
        for m in range(0 if k in DIRECT else 3, 7):
            rs(k, m).wait_recv()
            acc = acc + in_blocks[k, m].astype(F32)
        gate, upper, d_act = acc[:, 0:HALF], acc[:, HALF:HID], acc[:, HID:]
        sigma_v = jax.nn.sigmoid(gate)
        silu = gate * sigma_v
        home(k, 0)[:, 0:HALF] = (d_act * upper * sigma_v * (1.0 + gate * (1.0 - sigma_v))).astype(BF16)
        home(k, 0)[:, HALF:HID] = (d_act * silu).astype(BF16)
        home(k, 0)[:, HID:] = (silu * upper).astype(BF16)
        for m in range(7 if k in DIRECT else 4):
            ag(k, m).start()

    def stage_forward(k):
        ag(k, 0).wait_recv()
        ag(k, 4).start()
        ag(k, 5).start()
        ag(k, 1).wait_recv()
        ag(k, 6).start()

    def stage_back(k):
        for m in range(0 if k in DIRECT else 2, 7):
            ag(k, m).wait_recv()
        d_share(k).start()
        rows_grad = dot(rows_of(dall[0, own_blocks(k), :, 0:HID]), wgu[0], 1, 1)
        rows_grad = rows_grad + dot(rows_of(dall[1, own_blocks(k), :, 0:HID]), wgu[1], 1, 1)
        rg = rows_grad.reshape(SRC, CAP, 2 * FEAT)
        for cc in range(2):
            lo = cc * FEAT
            rsend[k, cc] = (
                jnp.concatenate([rg[:, :, lo:lo + 128], rg[:, :, lo + 128:lo + 256]], axis=1)
                .reshape(SRC * 16, 128).astype(BF16)
            )
        dst = ret.at[pl.ds(pl.multiple_of(ex * 16, 16), 16), :]
        for j, dz in enumerate(DZ[k]):
            for i in range(2):
                target = x_back[i] + z_at[(NZ - dz) % NZ]
                for cc in range(2):
                    src = rsend.at[k, cc, pl.ds((j * 2 + i) * 16, 16), :]
                    copy = pltpu.make_async_remote_copy(
                        src, dst, r_send, r_recv, device_id=(y * 2 + cc, target), device_id_type=MESH
                    )
                    if dz == 0 and i == 0 and cc == 0:
                        pl.when(c == 0)(pltpu.make_async_copy(src, dst, r_recv).start)
                        pl.when(c == 1)(copy.start)
                    else:
                        copy.start()

    stages = dict(D=stage_first, B=stage_relay, F=stage_point, H=stage_forward, E=stage_back)
    for _, k, name in ORDER:
        stages[name](k)

    for k in range(CHUNKS):
        x_share(k).wait_recv()
        xv, gv = split(rx[k, :, own_cols])
        xall[own_rows(k), :] = xv
        gall[own_rows(k), :] = gv
        xv, gv = split(xs[k])
        xall[sib_rows(k), :] = xv
        gall[sib_rows(k), :] = gv
    for k in range(CHUNKS):
        whole(dall.at[:, pl.ds(((1 - c) * CHUNKS + k) * 4, 4)], sh_recv.at[k])
    for hh in range(2):
        grads = rows_of(dall[hh])
        gu = dot(xall[...], grads[:, 0:HID], 0, 0).astype(BF16)
        g_gate[0, :, hh * HALF:(hh + 1) * HALF] = gu[:, 0:HALF]
        g_up[0, :, hh * HALF:(hh + 1) * HALF] = gu[:, HALF:]
        g_down[0, hh * HALF:(hh + 1) * HALF, :] = dot(grads[:, HID:], gall[...], 0, 0).astype(BF16)
    results = [
        pltpu.make_async_copy(v, h, o_sem.at[i])
        for i, (v, h) in enumerate(
            [(g_gate, g_gate_hbm), (g_up, g_up_hbm), (g_down, g_down_hbm), (g_tok, g_tok_hbm)]
        )
    ]
    for copy in results[:3]:
        copy.start()

    whole(ret, r_recv)
    both = dot(qt[...], ret[...], 1, 0)
    g_tok[:, 0:128] = both[0:TOK]
    g_tok[:, 128:] = both[TOK:]
    results[3].start()

    for copy in w_remote:
        copy.wait_send()
    whole(out_blocks, rs_send)
    whole(out_blocks, ag_send)
    whole(xs, x_send)
    whole(dall.at[:, pl.ds(0, 4 * CHUNKS)], sh_send)
    for source, sem in ((send, d_send), (ret, r_send)):
        pl.when(c == 0)(functools.partial(whole, source.at[pl.ds(0, EXPERTS * 16 - 16), :], sem))
        pl.when(c == 1)(functools.partial(whole, source, sem))
    for copy in results:
        copy.wait()


def hand_out(*refs):
    into, out = refs[12], refs[13]
    reads = [pltpu.make_async_copy(refs[i], refs[8 + i], into.at[i]) for i in range(4)]
    writes = [pltpu.make_async_copy(refs[8 + i], refs[4 + i], out.at[i]) for i in range(4)]
    for copy in reads:
        copy.start()
    for read, write in zip(reads, writes):
        read.wait()
        write.start()
    for copy in writes:
        copy.wait()


def local(tokens, out_grad, route_expert, route_weight, *weights):
    hbm = pl.BlockSpec(memory_space=pl.ANY)
    dma = pltpu.SemaphoreType.DMA
    shapes = (
        jax.ShapeDtypeStruct((TOK, FEAT), F32),
        jax.ShapeDtypeStruct((1, FEAT, HID), BF16),
        jax.ShapeDtypeStruct((1, FEAT, HID), BF16),
        jax.ShapeDtypeStruct((1, HID, FEAT), BF16),
    )
    found = pl.pallas_call(
        kernel,
        out_shape=shapes,
        in_specs=[hbm] * 7,
        out_specs=[hbm] * 4,
        scratch_shapes=[
            pltpu.VMEM((TOK, FEAT), BF16),
            pltpu.VMEM((TOK, FEAT), BF16),
            pltpu.VMEM((2, TOK), jnp.int32),
            pltpu.VMEM((2, TOK), F32),
            pltpu.VMEM((TOK, FEAT), F32),
            pltpu.VMEM((1, FEAT, HID), BF16),
            pltpu.VMEM((1, FEAT, HID), BF16),
            pltpu.VMEM((1, HID, FEAT), BF16),
            pltpu.VMEM((2, 2 * FEAT, HID), BF16),
            pltpu.VMEM((HID, 2 * FEAT), BF16),
            pltpu.VMEM((EXPERTS * 16, FEAT), BF16),
            pltpu.VMEM((2 * TOK, EXPERTS * 16), BF16),
            pltpu.VMEM((CHUNKS, SRC * 16, 2 * FEAT), BF16),
            pltpu.VMEM((CHUNKS, SRC * 16, FEAT), BF16),
            pltpu.VMEM((CHUNKS, 2 * ROWS, 3 * HALF), F32),
            pltpu.VMEM((CHUNKS, 7, 8, 3 * HALF), BF16),
            pltpu.VMEM((CHUNKS, 7, 8, 3 * HALF), BF16),
            pltpu.VMEM((2, 8 * CHUNKS, CAP, 3 * HALF), BF16),
            pltpu.VMEM((CHUNKS, 2, SRC * 16, 128), BF16),
            pltpu.VMEM((EXPERTS * 16, 128), BF16),
            pltpu.VMEM((2 * MINE, FEAT), BF16),
            pltpu.VMEM((2 * MINE, FEAT), BF16),
            dma((4,)), dma((4,)), dma((5,)), dma((5,)), dma((5,)),
            dma, dma((CHUNKS,)), dma, dma((CHUNKS,)),
            dma, dma((CHUNKS, 7)), dma, dma((CHUNKS, 7)),
            dma, dma((CHUNKS,)), dma, dma,
        ],
        compiler_params=pltpu.CompilerParams(
            collective_id=0, has_side_effects=True, vmem_limit_bytes=VMEM_LIMIT
        ),
        name="expert_backward",
    )(tokens, out_grad, route_expert.T, route_weight.T, *weights)
    return pl.pallas_call(
        hand_out,
        out_shape=shapes,
        in_specs=[hbm] * 4,
        out_specs=[hbm] * 4,
        scratch_shapes=[pltpu.VMEM(a.shape, a.dtype) for a in shapes] + [dma((4,)), dma((4,))],
        name="hand_out",
    )(*found)


def solution(mesh):
    in_specs = (
        P("expert", "dp"),
        P("expert", "dp"),
        P("expert", None),
        P("expert", None),
        P("expert", "dp", None),
        P("expert", "dp", None),
        P("expert", None, "dp"),
    )
    out_specs = (
        P("expert", "dp"),
        P("expert", "dp", None),
        P("expert", "dp", None),
        P("expert", None, "dp"),
    )
    return jax.shard_map(local, mesh=mesh, in_specs=in_specs, out_specs=out_specs, check_vma=False)
```

```python
import functools

import jax
import jax.numpy as jnp
from jax import lax
from jax.experimental import pallas as pl
from jax.experimental.pallas import tpu as pltpu
from jax.sharding import PartitionSpec as P

MESH = pl.DeviceIdType.MESH
NX, NZ, NY = 4, 16, 8
EXPERTS = NX * NZ
TOK, FEAT, HID, CAP = 128, 256, 768, 8
HALF = HID // 2
CHUNKS = 8
SRC = EXPERTS // 2 // CHUNKS
ROWS = SRC * CAP
MINE = CHUNKS * ROWS
LONG, SHORT = NY // 2, NY // 2 - 1
DZ = ((1, 15), (2, 14), (6, 10), (7, 9), (5, 11), (0, 8), (4, 12), (3, 13))
DIRECT = ()
DEPTH = 4
ORDER = (
    ("D", 0), ("D", 1), ("B", 0), ("D", 2), ("B", 1), ("F", 0), ("D", 3), ("B", 2), ("F", 1), ("D", 4),
    ("H", 0), ("B", 3), ("F", 2), ("H", 1), ("D", 5), ("B", 4), ("D", 6), ("F", 3), ("E", 0), ("H", 2),
    ("D", 7), ("B", 5), ("E", 1), ("F", 4), ("B", 6), ("H", 3), ("B", 7), ("E", 2), ("F", 5), ("H", 4),
    ("F", 6), ("E", 3), ("F", 7), ("H", 5), ("H", 6), ("E", 4), ("H", 7), ("E", 5), ("E", 6), ("E", 7),
)
VMEM_LIMIT = 60 * 1024 * 1024
F32, BF16 = jnp.float32, jnp.bfloat16


def dot(a, b, ca, cb):
    return lax.dot_general(a, b, (((ca,), (cb,)), ((), ())), preferred_element_type=F32)


def kernel(
    tok_hbm, og_hbm, rexp_hbm, rwt_hbm, wg, wu, wd,
    g_tok_hbm, g_gate_hbm, g_up_hbm, g_down_hbm,
    tok, og, rexp, rwt, g_tok, g_gate, g_up, g_down,
    wgu, wdn, send, qt, rx, xs, part, out_blocks, in_blocks, dall, rsend, ret, xall, gall,
    a_sem, o_sem, w_sem, ws_send, ws_recv, d_send, d_recv, x_send, x_recv,
    rs_send, rs_recv, ag_send, ag_recv, sh_send, sh_recv, r_send, r_recv,
):
    dp, ex = lax.axis_index("dp"), lax.axis_index("expert")
    y, c = lax.div(dp, 2), lax.rem(dp, 2)
    x, z = lax.div(ex, NZ), lax.rem(ex, NZ)
    sib = (y * 2 + 1 - c, ex)
    sigma = 1 - 2 * c

    small = [
        pltpu.make_async_copy(s, d, a_sem.at[i])
        for i, (s, d) in enumerate([(rexp_hbm, rexp), (rwt_hbm, rwt), (tok_hbm, tok), (og_hbm, og)])
    ]
    for copy in small:
        copy.start()

    x_at = [lax.rem(x + dx, NX) * NZ for dx in range(NX)]
    z_at = [lax.rem(z + dz, NZ) for dz in range(NZ)]
    y_at = {n: lax.rem(y + n * sigma + NY, NY) for n in range(-SHORT, LONG + 1)}
    x_even = [lax.rem(x + c + 2 * i, NX) * NZ for i in range(2)]
    x_odd = [lax.rem(x + 1 - c + 2 * i, NX) * NZ for i in range(2)]
    x_back = [lax.rem(x + 2 * NX - c - 2 * i, NX) * NZ for i in range(2)]

    def along_y(n):
        return (y_at[n] * 2 + c, ex)

    barrier = pltpu.get_barrier_semaphore()

    def signal(target):
        pl.semaphore_signal(barrier, inc=1, device_id=target, device_id_type=MESH)

    for dz in [8, 7, 9, 6, 10, 5, 11, 4, 12, 3, 13, 2, 14, 1, 15, 0]:
        for i in range(2):
            if dz == 0 and i == 0:
                pl.when(c == 1)(lambda: signal((y * 2, x_even[0] + z_at[0])))
            else:
                signal((y * 2, x_even[i] + z_at[dz]))
            signal((y * 2 + 1, x_even[i] + z_at[dz]))
            signal((y * 2 + 1 - c, x_odd[i] + z_at[dz]))
    for n in (4, 3, -3, 2, -2, 1, -1):
        signal(along_y(n))

    own_cols = pl.ds(pl.multiple_of(c * FEAT, FEAT), FEAT)
    sib_cols = pl.ds(pl.multiple_of((1 - c) * FEAT, FEAT), FEAT)

    def weight_parts():
        for hh in range(2):
            h_cols = pl.ds(hh * HALF, HALF)
            yield wg.at[0, :, h_cols], wgu.at[hh, own_cols, pl.ds(0, HALF)]
            yield wu.at[0, :, h_cols], wgu.at[hh, own_cols, pl.ds(HALF, HALF)]
        yield wd.at[0], wdn.at[:, own_cols]

    w_local = [pltpu.make_async_copy(s, d, w_sem.at[i]) for i, (s, d) in enumerate(weight_parts())]
    for copy in w_local:
        copy.start()
    for copy in small:
        copy.wait()

    lane = lax.broadcasted_iota(jnp.int32, (TOK, TOK), 1)
    sub = lax.broadcasted_iota(jnp.int32, (TOK, TOK), 0)
    ef, w = rexp[...].astype(F32), rwt[...]
    e0r, e1r = ef[0:1, :], ef[1:2, :]
    columns = jnp.where(
        sub == 0, e0r, jnp.where(sub == 1, e1r, jnp.where(sub == 2, w[0:1, :], w[1:2, :]))
    ).T
    e0c, e1c, w0c, w1c = columns[:, 0:1], columns[:, 1:2], columns[:, 2:3], columns[:, 3:4]
    slots = 2 * EXPERTS * CAP
    si = lax.broadcasted_iota(jnp.int32, (slots, TOK), 0)
    s_exp = (si // (2 * CAP)).astype(F32)
    s_rank = (si % CAP).astype(F32)
    s_cot = (si % (2 * CAP)) >= CAP
    m0 = (s_exp == e0r).astype(F32)
    m1 = (s_exp == e1r).astype(F32)
    rank = dot((m0 + m1).astype(BF16), (sub < lane).astype(BF16), 1, 0)
    hit = rank == s_rank
    zero = jnp.zeros_like(m0)
    p0 = jnp.where(hit, m0, zero)
    p1 = jnp.where(hit, m1, zero)
    onehot = jnp.concatenate(
        [jnp.where(s_cot, zero, p0 + p1), jnp.where(s_cot, p0, zero), jnp.where(s_cot, p1, zero)], axis=1
    ).astype(BF16)
    o = og[...].astype(F32)
    g0 = (w0c * o).astype(BF16)
    g1 = (w1c * o).astype(BF16)
    values = jnp.concatenate([tok[...], g0, g1], axis=0)
    send[...] = dot(onehot, values, 1, 0).astype(BF16)

    pl.semaphore_wait(barrier, 102 + c)

    def dispatch(k):
        for j, dz in enumerate(DZ[k]):
            for dx in range(NX):
                target = x_at[dx] + z_at[dz]
                src = send.at[pl.ds(pl.multiple_of(target * 16, 16), 16), :]
                dst = rx.at[k, pl.ds((j * 2 + dx // 2) * 16, 16), own_cols]
                copy = pltpu.make_async_remote_copy(
                    src, dst, d_send, d_recv.at[k],
                    device_id=(y * 2 + dx % 2, target), device_id_type=MESH,
                )
                if dx == 0 and dz == 0:
                    pl.when(c == 0)(pltpu.make_async_copy(src, dst, d_recv.at[k]).start)
                    pl.when(c == 1)(copy.start)
                else:
                    copy.start()

    dispatch(0)
    w_remote = [
        pltpu.make_async_remote_copy(
            s, d, ws_send.at[i], ws_recv.at[i], device_id=sib, device_id_type=MESH
        )
        for i, (s, d) in enumerate(weight_parts())
    ]
    for copy in w_remote:
        copy.start()
    for k in range(1, DEPTH):
        dispatch(k)

    ti = lax.broadcasted_iota(jnp.int32, (TOK, slots), 1)
    t_exp = (ti // (2 * CAP)).astype(F32)
    t_rank = (ti % CAP).astype(F32)
    t_cot = (ti % (2 * CAP)) >= CAP
    tm = (t_exp == e0c).astype(F32) + (t_exp == e1c).astype(F32)
    trank = dot((lane < sub).astype(BF16), tm.astype(BF16), 1, 0)
    tz = jnp.zeros_like(tm)
    tp = jnp.where(trank == t_rank, tm, tz)
    qt[0:TOK, :] = jnp.where(t_cot, tz, tp).astype(BF16)
    qt[TOK:, :] = jnp.where(t_cot, tp, tz).astype(BF16)

    for copy in w_local:
        copy.wait()

    def whole(ref, sem):
        pltpu.make_async_copy(ref, ref, sem).wait()

    def split(rows16):
        v = rows16.astype(F32)
        width = v.shape[1]
        v = v.reshape(SRC, 2, CAP, width)
        return v[:, 0].reshape(ROWS, width).astype(BF16), v[:, 1].reshape(ROWS, width).astype(BF16)

    def rows_of(blocks):
        return blocks.astype(F32).reshape(blocks.shape[0] * CAP, blocks.shape[2]).astype(BF16)

    RS_TO = [2, 1, -1, 1, -1, 2, -2]
    RS_FOR = [4, 3, -3, 1, -1, 2, -2]
    RS_ADD = {5: (0, 1), 6: (2,)}
    FAR_FIRST = [4, 3, -3, 2, -2, 1, -1]

    def block(k, n):
        return part[k, pl.ds(pl.multiple_of(y_at[n] * 8, 8), 8), :]

    def rs(k, m):
        return pltpu.make_async_remote_copy(
            out_blocks.at[k, m], in_blocks.at[k, m], rs_send, rs_recv.at[k, m],
            device_id=along_y((FAR_FIRST if k in DIRECT else RS_TO)[m]), device_id_type=MESH,
        )

    AG_TO = [2, -2, 1, -1, 1, 2, -1]
    AG_OF = [0, 0, 0, 0, -2, -2, 2]

    def home(k, n):
        who = y_at[n]
        return dall.at[lax.div(who, 4), (c * CHUNKS + k) * 4 + lax.rem(who, 4)]

    def ag(k, m):
        ref = home(k, 0 if k in DIRECT else AG_OF[m])
        to = along_y((FAR_FIRST if k in DIRECT else AG_TO)[m])
        return pltpu.make_async_remote_copy(
            ref, ref, ag_send, ag_recv.at[k, m], device_id=to, device_id_type=MESH
        )

    def x_share(k):
        return pltpu.make_async_remote_copy(
            rx.at[k, :, sib_cols], xs.at[k], x_send, x_recv.at[k], device_id=sib, device_id_type=MESH
        )

    def own_rows(k):
        return pl.ds(pl.multiple_of(c * MINE + k * ROWS, ROWS), ROWS)

    def sib_rows(k):
        return pl.ds(pl.multiple_of((1 - c) * MINE + k * ROWS, ROWS), ROWS)

    def own_blocks(k):
        return pl.ds((c * CHUNKS + k) * 4, 4)

    def d_share(k):
        ref = dall.at[:, own_blocks(k)]
        return pltpu.make_async_remote_copy(
            ref, ref, sh_send, sh_recv.at[k], device_id=sib, device_id_type=MESH
        )

    def stage_first(k):
        whole(rx.at[k], d_recv.at[k])
        if k + DEPTH < CHUNKS:
            dispatch(k + DEPTH)
        if k == 0:
            for copy in w_remote:
                copy.wait_recv()
        xv, gv = split(rx[k])
        for hh in range(2):
            part[k, hh * ROWS:(hh + 1) * ROWS, 0:HID] = dot(xv, wgu[hh], 1, 0)
            part[k, hh * ROWS:(hh + 1) * ROWS, HID:] = dot(gv, wdn[hh * HALF:(hh + 1) * HALF, :], 1, 1)
        for m in range(7 if k in DIRECT else 5):
            out_blocks[k, m] = block(k, (FAR_FIRST if k in DIRECT else RS_FOR)[m]).astype(BF16)
            rs(k, m).start()
        x_share(k).start()

    def stage_relay(k):
        for m in (5, 6):
            acc = block(k, RS_FOR[m])
            for n in RS_ADD[m]:
                rs(k, n).wait_recv()
                acc = acc + in_blocks[k, n].astype(F32)
            out_blocks[k, m] = acc.astype(BF16)
            rs(k, m).start()

    def stage_point(k):
        acc = block(k, 0)
        for m in range(0 if k in DIRECT else 3, 7):
            rs(k, m).wait_recv()
            acc = acc + in_blocks[k, m].astype(F32)
        gate, upper, d_act = acc[:, 0:HALF], acc[:, HALF:HID], acc[:, HID:]
        sigma_v = jax.nn.sigmoid(gate)
        silu = gate * sigma_v
        home(k, 0)[:, 0:HALF] = (d_act * upper * sigma_v * (1.0 + gate * (1.0 - sigma_v))).astype(BF16)
        home(k, 0)[:, HALF:HID] = (d_act * silu).astype(BF16)
        home(k, 0)[:, HID:] = (silu * upper).astype(BF16)
        for m in range(7 if k in DIRECT else 4):
            ag(k, m).start()

    def stage_forward(k):
        ag(k, 0).wait_recv()
        ag(k, 4).start()
        ag(k, 5).start()
        ag(k, 1).wait_recv()
        ag(k, 6).start()

    def stage_back(k):
        for m in range(0 if k in DIRECT else 2, 7):
            ag(k, m).wait_recv()
        rows_grad = dot(rows_of(dall[0, own_blocks(k), :, 0:HID]), wgu[0], 1, 1)
        rows_grad = rows_grad + dot(rows_of(dall[1, own_blocks(k), :, 0:HID]), wgu[1], 1, 1)
        rg = rows_grad.reshape(SRC, CAP, 2 * FEAT)
        for cc in range(2):
            lo = cc * FEAT
            rsend[k, cc] = (
                jnp.concatenate([rg[:, :, lo:lo + 128], rg[:, :, lo + 128:lo + 256]], axis=1)
                .reshape(SRC * 16, 128).astype(BF16)
            )
        dst = ret.at[pl.ds(pl.multiple_of(ex * 16, 16), 16), :]
        for j, dz in enumerate(DZ[k]):
            for i in range(2):
                target = x_back[i] + z_at[(NZ - dz) % NZ]
                for cc in range(2):
                    src = rsend.at[k, cc, pl.ds((j * 2 + i) * 16, 16), :]
                    copy = pltpu.make_async_remote_copy(
                        src, dst, r_send, r_recv, device_id=(y * 2 + cc, target), device_id_type=MESH
                    )
                    if dz == 0 and i == 0 and cc == 0:
                        pl.when(c == 0)(pltpu.make_async_copy(src, dst, r_recv).start)
                        pl.when(c == 1)(copy.start)
                    else:
                        copy.start()
        d_share(k).start()

    stages = dict(D=stage_first, B=stage_relay, F=stage_point, H=stage_forward, E=stage_back)
    for name, k in ORDER:
        stages[name](k)

    for k in range(CHUNKS):
        x_share(k).wait_recv()
        xv, gv = split(rx[k, :, own_cols])
        xall[own_rows(k), :] = xv
        gall[own_rows(k), :] = gv
        xv, gv = split(xs[k])
        xall[sib_rows(k), :] = xv
        gall[sib_rows(k), :] = gv
    for k in range(CHUNKS):
        whole(dall.at[:, pl.ds(((1 - c) * CHUNKS + k) * 4, 4)], sh_recv.at[k])
    for hh in range(2):
        grads = rows_of(dall[hh])
        gu = dot(xall[...], grads[:, 0:HID], 0, 0).astype(BF16)
        g_gate[0, :, hh * HALF:(hh + 1) * HALF] = gu[:, 0:HALF]
        g_up[0, :, hh * HALF:(hh + 1) * HALF] = gu[:, HALF:]
        g_down[0, hh * HALF:(hh + 1) * HALF, :] = dot(grads[:, HID:], gall[...], 0, 0).astype(BF16)
    results = [
        pltpu.make_async_copy(v, h, o_sem.at[i])
        for i, (v, h) in enumerate(
            [(g_gate, g_gate_hbm), (g_up, g_up_hbm), (g_down, g_down_hbm), (g_tok, g_tok_hbm)]
        )
    ]
    for copy in results[:3]:
        copy.start()

    whole(ret, r_recv)
    both = dot(qt[...], ret[...], 1, 0)
    g_tok[:, 0:128] = both[0:TOK]
    g_tok[:, 128:] = both[TOK:]
    results[3].start()

    for copy in w_remote:
        copy.wait_send()
    whole(out_blocks, rs_send)
    whole(out_blocks, ag_send)
    whole(xs, x_send)
    whole(dall.at[:, pl.ds(0, 4 * CHUNKS)], sh_send)
    for source, sem in ((send, d_send), (ret, r_send)):
        pl.when(c == 0)(functools.partial(whole, source.at[pl.ds(0, EXPERTS * 16 - 16), :], sem))
        pl.when(c == 1)(functools.partial(whole, source, sem))
    for copy in results:
        copy.wait()


def hand_out(*refs):
    into, out = refs[12], refs[13]
    reads = [pltpu.make_async_copy(refs[i], refs[8 + i], into.at[i]) for i in range(4)]
    writes = [pltpu.make_async_copy(refs[8 + i], refs[4 + i], out.at[i]) for i in range(4)]
    for copy in reads:
        copy.start()
    for read, write in zip(reads, writes):
        read.wait()
        write.start()
    for copy in writes:
        copy.wait()


def local(tokens, out_grad, route_expert, route_weight, *weights):
    hbm = pl.BlockSpec(memory_space=pl.ANY)
    dma = pltpu.SemaphoreType.DMA
    shapes = (
        jax.ShapeDtypeStruct((TOK, FEAT), F32),
        jax.ShapeDtypeStruct((1, FEAT, HID), BF16),
        jax.ShapeDtypeStruct((1, FEAT, HID), BF16),
        jax.ShapeDtypeStruct((1, HID, FEAT), BF16),
    )
    found = pl.pallas_call(
        kernel,
        out_shape=shapes,
        in_specs=[hbm] * 7,
        out_specs=[hbm] * 4,
        scratch_shapes=[
            pltpu.VMEM((TOK, FEAT), BF16),
            pltpu.VMEM((TOK, FEAT), BF16),
            pltpu.VMEM((2, TOK), jnp.int32),
            pltpu.VMEM((2, TOK), F32),
            pltpu.VMEM((TOK, FEAT), F32),
            pltpu.VMEM((1, FEAT, HID), BF16),
            pltpu.VMEM((1, FEAT, HID), BF16),
            pltpu.VMEM((1, HID, FEAT), BF16),
            pltpu.VMEM((2, 2 * FEAT, HID), BF16),
            pltpu.VMEM((HID, 2 * FEAT), BF16),
            pltpu.VMEM((EXPERTS * 16, FEAT), BF16),
            pltpu.VMEM((2 * TOK, EXPERTS * 16), BF16),
            pltpu.VMEM((CHUNKS, SRC * 16, 2 * FEAT), BF16),
            pltpu.VMEM((CHUNKS, SRC * 16, FEAT), BF16),
            pltpu.VMEM((CHUNKS, 2 * ROWS, 3 * HALF), F32),
            pltpu.VMEM((CHUNKS, 7, 8, 3 * HALF), BF16),
            pltpu.VMEM((CHUNKS, 7, 8, 3 * HALF), BF16),
            pltpu.VMEM((2, 8 * CHUNKS, CAP, 3 * HALF), BF16),
            pltpu.VMEM((CHUNKS, 2, SRC * 16, 128), BF16),
            pltpu.VMEM((EXPERTS * 16, 128), BF16),
            pltpu.VMEM((2 * MINE, FEAT), BF16),
            pltpu.VMEM((2 * MINE, FEAT), BF16),
            dma((4,)), dma((4,)), dma((5,)), dma((5,)), dma((5,)),
            dma, dma((CHUNKS,)), dma, dma((CHUNKS,)),
            dma, dma((CHUNKS, 7)), dma, dma((CHUNKS, 7)),
            dma, dma((CHUNKS,)), dma, dma,
        ],
        compiler_params=pltpu.CompilerParams(
            collective_id=0, has_side_effects=True, vmem_limit_bytes=VMEM_LIMIT
        ),
        name="expert_backward",
    )(tokens, out_grad, route_expert.T, route_weight.T, *weights)
    return pl.pallas_call(
        hand_out,
        out_shape=shapes,
        in_specs=[hbm] * 4,
        out_specs=[hbm] * 4,
        scratch_shapes=[pltpu.VMEM(a.shape, a.dtype) for a in shapes] + [dma((4,)), dma((4,))],
        name="hand_out",
    )(*found)


def solution(mesh):
    in_specs = (
        P("expert", "dp"),
        P("expert", "dp"),
        P("expert", None),
        P("expert", None),
        P("expert", "dp", None),
        P("expert", "dp", None),
        P("expert", None, "dp"),
    )
    out_specs = (
        P("expert", "dp"),
        P("expert", "dp", None),
        P("expert", "dp", None),
        P("expert", None, "dp"),
    )
    return jax.shard_map(local, mesh=mesh, in_specs=in_specs, out_specs=out_specs, check_vma=False)
```
